32 devices in a mesh: groups: 2 (over x), wide: 16 (over z, y, core).
Axes of the slice: x: 2, y: 2, z: 4, core: 2. Of those that a mesh axis runs over, the one named last changes fastest.
Arguments:
- voltages: bfloat16 [512, 265216], P('wide', 'groups'), parts along dimension 1, may hold values from -6 to 6
- antenna_flags: int32 [1024], P(('groups', 'wide')), parts along dimension 0, may hold values 0 or 1
- baseline_pairs: int32 [2, 2048], replicated, may hold values from 0 to 511, as said below
Outputs:
- delay_power: float32 [512, 2048], P('groups', 'wide'), parts along dimension 0
The draws below stay inside these ranges and needn't reach their ends.
There are 2 independent parts, one for each index of `groups`. The reference program is written for one: setup_inputs(seed, part) draws one part's arguments, and reference() takes and returns one part's arrays. A program takes and returns all parts, laid end to end along the dimension named above; an argument that names none is the same for every part. Nothing has to cross between parts.
Inputs may be any that keep to these rules, and one draw needn't show every extreme that they name: `baseline_pairs`: the two inputs of a baseline always differ; baseline 0 pairs input 0 with input 512 - 1.
All inputs are finite; a program needn't handle non-finite values. No bound on the sum of `antenna_flags` on one device may be relied on, other than what follows from the above.
Results may differ from the reference program's by a relative error of at most 0.0055.
Values may be sent and summed in bfloat16 or wider, within the bound.
A program may use at most 192 MiB of HBM per device.

```python
import math
import jax
import jax.numpy as jnp
from jax import lax

INPUT_COUNT = 512
CHANNEL_COUNT = 256
TAPS = 4
NT = 128
NFFT = 512
SAMPLES = 132608
BASELINE_TOTAL = 2048


def draw_baseline_pairs(key, part):
    leading_key = jax.random.fold_in(key, 11)
    trailing_key = jax.random.fold_in(key, 23)
    first_input = jax.random.randint(leading_key, (BASELINE_TOTAL,), 0, INPUT_COUNT, dtype=jnp.int32)
    start_shift = jax.random.randint(trailing_key, (BASELINE_TOTAL,), 1, INPUT_COUNT, dtype=jnp.int32)
    first_input = first_input.at[0].set(0)
    start_shift = start_shift.at[0].set(INPUT_COUNT - 1)
    second = (first_input + start_shift) % INPUT_COUNT
    return jnp.stack([first_input, second], axis=0).astype(jnp.int32)


def place_ends(array, rng, smallest, largest):
    longest = array.shape.index(max(array.shape))
    spots = []
    for shift in (0, 1):
        where = [jax.random.randint(jax.random.fold_in(rng, axis), (), 0, length) for axis, length in enumerate(array.shape)]
        where[longest] = (where[longest] + shift) % array.shape[longest]
        spots.append(tuple(where))
    return array.at[spots[0]].set(smallest).at[spots[1]].set(largest)


def levels(stream_key, dims, cuts, smallest, top_value):
    level, own = 1.0, jax.random.fold_in(stream_key, 6)
    for axis_at, parts in cuts:
        heights = jnp.exp(jax.random.uniform(jax.random.fold_in(own, axis_at), (parts,), jnp.float32, smallest / len(cuts), top_value / len(cuts)))
        level = level * jnp.repeat(heights, dims[axis_at] // parts).reshape([-1 if axis == axis_at else 1 for axis in range(len(dims))])
    return level


def scatter_about(key, extent, deviation, limit, split=(), kind=jnp.bfloat16):
    entries = jax.random.normal(key, extent, jnp.float32) * deviation
    if len(split) > 0:
        entries = levels(key, extent, split, -0.22, 0.18) * entries
    return jnp.clip(entries, min=-limit, max=limit).astype(kind)


def setup_inputs(seed: int = 0, part: int = 0) -> dict:
    streams_of = jax.random.split(jax.random.key(seed), 4)
    own_keys = jax.random.split(jax.random.fold_in(streams_of[3], part), 4)
    voltages = scatter_about(own_keys[0], (INPUT_COUNT, SAMPLES), 1.0, 6.0, ((0, 16),))
    antenna_flags = place_ends((jax.random.randint(own_keys[1], (INPUT_COUNT,), 0, 8) < 7).astype(jnp.int32), jax.random.fold_in(own_keys[1], 1), 0, 1)
    baseline_pairs = draw_baseline_pairs(jax.random.fold_in(streams_of[3], 71), part)
    return dict(voltages=voltages, antenna_flags=antenna_flags, baseline_pairs=baseline_pairs)


def prototype_table():
    count = TAPS * NFFT
    positions = jnp.arange(count, dtype=jnp.float32)
    start_shift = (positions - count / 2 + 0.5) / NFFT
    hamming = 0.54 - 0.46 * jnp.cos(2 * jnp.pi * positions / (count - 1))
    return (jnp.sinc(start_shift) * hamming).reshape(TAPS, NFFT)

def filter_bank(voltages, antenna_flags, first_input, count):
    framed = voltages.astype(jnp.float32).reshape(voltages.shape[0], -1, NFFT)
    prototype = prototype_table()
    filtered = jnp.zeros((voltages.shape[0], count, NFFT), jnp.float32)
    for tap_index in range(TAPS):
        filtered = filtered + prototype[tap_index][None, None, :] * framed[:, first_input + tap_index:first_input + tap_index + count, :]
    return filtered * antenna_flags.astype(jnp.float32)[:, None, None]

def delay_table():
    chan_int = jnp.arange(CHANNEL_COUNT, dtype=jnp.int32)
    chan_float = chan_int.astype(jnp.float32)
    base = 2 * jnp.pi * chan_float / (CHANNEL_COUNT - 1)
    window = 0.35875 - 0.48829 * jnp.cos(base) + 0.14128 * jnp.cos(2 * base) - 0.01168 * jnp.cos(3 * base)
    phase = chan_int[:, None] * chan_int[None, :] % CHANNEL_COUNT
    angle = 2 * jnp.pi * phase.astype(jnp.float32) / CHANNEL_COUNT
    cosine = jnp.cos(angle) * window[None, :]
    sine = jnp.sin(angle) * window[None, :]
    upper = jnp.concatenate([cosine, sine], axis=1)
    lower = jnp.concatenate([-sine, cosine], axis=1)
    table = jnp.concatenate([upper, lower], axis=0) / jnp.sqrt(jnp.sum(window * window))
    return table.astype(jnp.bfloat16)

def reference(voltages, antenna_flags, baseline_pairs):
    filtered = filter_bank(voltages, antenna_flags, 0, 2 * NT)
    spectrum = jnp.fft.rfft(filtered, axis=-1)[..., :CHANNEL_COUNT] / math.sqrt(NFFT)
    real_part = jnp.real(spectrum).astype(jnp.bfloat16)
    imag_part = jnp.imag(spectrum).astype(jnp.bfloat16)
    by_channel = jnp.transpose(jnp.stack([real_part, imag_part]), (3, 0, 1, 2))
    flat_index = (baseline_pairs[0] * INPUT_COUNT + baseline_pairs[1]).astype(jnp.int32)
    scale = 1.0 / math.sqrt(2 * NT)

    def one_channel(block):
        values = block.astype(jnp.float32)
        total = jnp.zeros((2, INPUT_COUNT, INPUT_COUNT), jnp.float32)
        for batch_index in range(2):
            part = values[:, :, batch_index * NT:(batch_index + 1) * NT]
            swapped = jnp.stack([part[1], -part[0]])
            stacked = jnp.stack([part, swapped])
            total = total + jnp.einsum('qrit,rjt->qij', stacked, part, precision=lax.Precision.HIGHEST)
        picked = total.reshape(2, INPUT_COUNT * INPUT_COUNT)[:, flat_index] * scale
        return picked.astype(jnp.bfloat16)
    cross_visibility = lax.map(one_channel, by_channel)
    column_list = jnp.transpose(cross_visibility, (1, 0, 2)).reshape(2 * CHANNEL_COUNT, BASELINE_TOTAL)
    delays = jnp.dot(delay_table(), column_list, preferred_element_type=jnp.float32)
    return delays[:CHANNEL_COUNT] ** 2 + delays[CHANNEL_COUNT:] ** 2
```

```python
import functools
import math

import jax
import jax.numpy as jnp
import ml_dtypes
import numpy as np
from jax import lax
from jax.experimental import pallas as pl
from jax.experimental.pallas import tpu as pltpu
from jax.sharding import PartitionSpec as P

INPUT_COUNT = 512
CHANNEL_COUNT = 256
TAPS = 4
NT = 128
NFFT = 512


def prototype_table():
    count = TAPS * NFFT
    positions = jnp.arange(count, dtype=jnp.float32)
    start_shift = (positions - count / 2 + 0.5) / NFFT
    hamming = 0.54 - 0.46 * jnp.cos(2 * jnp.pi * positions / (count - 1))
    return (jnp.sinc(start_shift) * hamming).reshape(TAPS, NFFT)


def filter_bank(voltages, antenna_flags, first_input, count):
    framed = voltages.astype(jnp.float32).reshape(voltages.shape[0], -1, NFFT)
    prototype = prototype_table()
    filtered = jnp.zeros((voltages.shape[0], count, NFFT), jnp.float32)
    for tap_index in range(TAPS):
        filtered = (
            filtered
            + prototype[tap_index][None, None, :]
            * framed[:, first_input + tap_index : first_input + tap_index + count, :]
        )
    return filtered * antenna_flags.astype(jnp.float32)[:, None, None]


def transform_table():
    rows_int = jnp.arange(2 * CHANNEL_COUNT, dtype=jnp.int32)
    channel = rows_int // 2
    is_real = rows_int % 2 == 0
    sample = jnp.arange(NFFT, dtype=jnp.int32)
    phase = channel[:, None] * sample[None, :] % NFFT
    angle = 2 * jnp.pi * phase.astype(jnp.float32) / NFFT
    table = jnp.where(is_real[:, None], jnp.cos(angle), -jnp.sin(angle))
    return table / math.sqrt(NFFT)


def delay_table():
    chan_int = jnp.arange(CHANNEL_COUNT, dtype=jnp.int32)
    chan_float = chan_int.astype(jnp.float32)
    base = 2 * jnp.pi * chan_float / (CHANNEL_COUNT - 1)
    window = (
        0.35875
        - 0.48829 * jnp.cos(base)
        + 0.14128 * jnp.cos(2 * base)
        - 0.01168 * jnp.cos(3 * base)
    )
    phase = chan_int[:, None] * chan_int[None, :] % CHANNEL_COUNT
    angle = 2 * jnp.pi * phase.astype(jnp.float32) / CHANNEL_COUNT
    cosine = jnp.cos(angle) * window[None, :]
    sine = jnp.sin(angle) * window[None, :]
    upper = jnp.concatenate([cosine, sine], axis=1)
    lower = jnp.concatenate([-sine, cosine], axis=1)
    table = jnp.concatenate([upper, lower], axis=0) / jnp.sqrt(jnp.sum(window * window))
    return table.astype(jnp.bfloat16)


def correlate(received):
    values = received[0]
    swapped = jnp.stack([values[:, 1], -values[:, 0]], axis=1)
    stacked = jnp.stack([values, swapped], axis=0)
    return jnp.einsum("qcrit,crjt->iqcj", stacked, values, preferred_element_type=jnp.float32)


def per_device_general(voltages, antenna_flags, baseline_pairs):
    width = lax.axis_size("wide")
    local_inputs = voltages.shape[0]
    local_channels = CHANNEL_COUNT // width
    table = transform_table()
    scale = 1.0 / math.sqrt(2 * NT)
    correlation = jnp.zeros((INPUT_COUNT, 2, local_channels, INPUT_COUNT), jnp.float32)
    for batch_index in range(2):
        filtered = filter_bank(voltages, antenna_flags, batch_index * NT, NT)
        raw = jnp.einsum(
            "kn,itn->kit",
            table,
            filtered,
            precision=lax.Precision.HIGHEST,
            preferred_element_type=jnp.float32,
        )
        correlation = correlation + correlate(
            lax.all_to_all(
                raw.astype(jnp.bfloat16).reshape(width, local_channels, 2, local_inputs, NT),
                "wide",
                split_axis=0,
                concat_axis=3,
                tiled=True,
            )
        )
    baseline_count = baseline_pairs.shape[1]
    block_size = math.gcd(baseline_count, 1024)
    first_blocks = baseline_pairs[0].reshape(baseline_count // block_size, block_size)
    second_blocks = baseline_pairs[1].reshape(baseline_count // block_size, block_size)
    input_positions = jnp.arange(INPUT_COUNT, dtype=jnp.int32)

    def select_block(indices):
        first_block, second_block = indices
        rows_taken = jnp.take(correlation, first_block, axis=0)
        selector = (input_positions[None, :] == second_block[:, None]).astype(jnp.float32)
        return jnp.sum(rows_taken * selector[:, None, None, :], axis=3)

    selected = lax.map(select_block, (first_blocks, second_blocks))
    selected = selected.reshape(baseline_count, 2, local_channels)
    picked = (jnp.transpose(selected, (1, 2, 0)) * scale).astype(jnp.bfloat16)
    regrouped = lax.all_to_all(picked, "wide", split_axis=2, concat_axis=1, tiled=True)
    column_list = regrouped.reshape(2 * CHANNEL_COUNT, regrouped.shape[2])
    delays = jnp.dot(delay_table(), column_list, preferred_element_type=jnp.float32)
    return delays[:CHANNEL_COUNT] ** 2 + delays[CHANNEL_COUNT:] ** 2


LANES = 128
HALF = NFFT // 2
PIECES = 4
STEP = 4


def owned_channels(width):
    each = CHANNEL_COUNT // width // 2
    owner = np.arange(width)[:, None, None]
    parity = np.arange(2)[None, :, None]
    return 2 * (owner * each + np.arange(each)[None, None, :]) + parity


def split_transform_table(width):
    channel = owned_channels(width).transpose(1, 0, 2)[:, :, None, :, None]
    angle = 2 * np.pi * (channel * np.arange(HALF) % NFFT) / NFFT
    table = np.concatenate([np.cos(angle), -np.sin(angle)], axis=2) / math.sqrt(NFFT)
    table = table.reshape(2, -1, HALF).astype(np.float32)
    high = table.astype(ml_dtypes.bfloat16)
    low = (table - high.astype(np.float32)).astype(ml_dtypes.bfloat16)
    return np.concatenate([high, high, low], axis=2)


def ordered_delay_table(width):
    chan = np.arange(CHANNEL_COUNT)
    base = 2 * np.pi * chan / (CHANNEL_COUNT - 1)
    window = (
        0.35875 - 0.48829 * np.cos(base) + 0.14128 * np.cos(2 * base) - 0.01168 * np.cos(3 * base)
    )
    angle = 2 * np.pi * (chan[:, None] * chan[None, :] % CHANNEL_COUNT) / CHANNEL_COUNT
    cosine, sine = np.cos(angle) * window, np.sin(angle) * window
    table = np.block([[cosine, sine], [-sine, cosine]]) / np.sqrt(np.sum(window * window))
    channel = owned_channels(width)[:, :, None, :]
    order = channel + CHANNEL_COUNT * np.arange(2)[None, None, :, None]
    return table[:, order.reshape(-1)].astype(np.float32).astype(ml_dtypes.bfloat16)


def spectra_kernel(batch, volts, flags, proto, table, out, held, filt, sems):
    inputs = held.shape[0]
    piece = NT // PIECES
    copies = []
    for part in range(PIECES):
        frames = piece + (TAPS - 1 if part == PIECES - 1 else 0)
        copies.append(
            pltpu.make_async_copy(
                volts.at[:, pl.ds((batch * NT + part * piece) * NFFT, frames * NFFT)],
                held.at[:, pl.ds(part * piece * NFFT, frames * NFFT)],
                sems.at[part],
            )
        )
    for copy in copies:
        copy.start()
    copies[0].wait()
    for part in range(PIECES):
        if part + 1 < PIECES:
            copies[part + 1].wait()

        @pl.loop(part * piece // STEP, (part + 1) * piece // STEP)
        def _(step):
            first = step * STEP
            flag = flags[...]
            for block in range(2):
                sides = []
                for lane in (block * LANES, HALF + block * LANES):
                    frames = [
                        held[
                            :, pl.ds(pl.multiple_of((first + f) * NFFT + lane, LANES), LANES)
                        ].astype(jnp.float32)
                        for f in range(STEP + TAPS - 1)
                    ]
                    weights = [proto[tap : tap + 1, lane : lane + LANES] for tap in range(TAPS)]
                    sides.append(
                        [
                            sum(weights[tap] * frames[u + tap] for tap in range(TAPS)) * flag
                            for u in range(STEP)
                        ]
                    )
                for u in range(STEP):
                    rows = pl.ds(pl.multiple_of((first + u) * inputs, 8), inputs)
                    filt[block, rows, :] = sides[0][u] + sides[1][u]
                    filt[2 + block, rows, :] = sides[0][u] - sides[1][u]

    rows_each = out.shape[2] // 2

    @pl.loop(0, inputs, unroll=2)
    def _(a):
        for parity in range(2):
            x = jnp.concatenate(
                [filt[2 * parity + b, pl.ds(a, NT, stride=inputs), :] for b in range(2)], axis=1
            )
            high = x.astype(jnp.bfloat16)
            low = (x - high.astype(jnp.float32)).astype(jnp.bfloat16)
            result = lax.dot_general(
                table[parity],
                jnp.concatenate([high, low, high], axis=1),
                (((1,), (1,)), ((), ())),
                preferred_element_type=jnp.float32,
            )
            out[:, a, parity * rows_each : (parity + 1) * rows_each, :] = result.astype(
                jnp.bfloat16
            ).reshape(out.shape[0], rows_each, NT)


def make_spectra(batch, voltages, flags, proto, table, width):
    inputs = voltages.shape[0]
    rows = 2 * CHANNEL_COUNT // width
    vmem = pl.BlockSpec(memory_space=pltpu.VMEM)
    return pl.pallas_call(
        functools.partial(spectra_kernel, batch),
        out_shape=jax.ShapeDtypeStruct((width, inputs, rows, NT), jnp.bfloat16),
        in_specs=[pl.BlockSpec(memory_space=pl.ANY), vmem, vmem, vmem],
        out_specs=vmem,
        scratch_shapes=[
            pltpu.VMEM((inputs, (NT + TAPS - 1) * NFFT), jnp.bfloat16),
            pltpu.VMEM((4, NT * inputs, LANES), jnp.float32),
            pltpu.SemaphoreType.DMA((PIECES,)),
        ],
        compiler_params=pltpu.CompilerParams(vmem_limit_bytes=40 * 2**20),
        cost_estimate=pl.CostEstimate(
            flops=6 * 2 * CHANNEL_COUNT * HALF * NT * inputs,
            bytes_accessed=4 * NT * NFFT * inputs,
            transcendentals=0,
        ),
        name="spectra",
    )(voltages, flags, proto, table)


def baseline_kernel(last, pairs, values, *rest):
    before, out = rest if last else (None, rest[0])
    rows = values.shape[1]
    each = rows // 4
    lane = lax.broadcasted_iota(jnp.int32, (rows, LANES), 1)

    @pl.loop(0, out.shape[0])
    def _(block):
        def one(at, total):
            k = block * LANES + at
            a = values[pairs[0, k]].astype(jnp.float32)
            b = values[pairs[1, k]].astype(jnp.float32)
            products = []
            for start in (0, 2 * each):
                a_re, a_im = a[start : start + each], a[start + each : start + 2 * each]
                b_re, b_im = b[start : start + each], b[start + each : start + 2 * each]
                products.append(a_re * b_re + a_im * b_im)
                products.append(a_im * b_re - a_re * b_im)
            summed = jnp.sum(jnp.concatenate(products, axis=0), axis=1, keepdims=True)
            return jnp.where(lane == at, summed, total)

        total = lax.fori_loop(0, LANES, one, jnp.zeros((rows, LANES), jnp.float32), unroll=8)
        if last:
            total = (total + before[block]) * (1.0 / math.sqrt(2 * NT))
        out[block] = total.astype(out.dtype)


def correlate_baselines(pairs, values, before=None):
    last = before is not None
    count, rows = pairs.shape[1], values.shape[1]
    vmem = pl.BlockSpec(memory_space=pltpu.VMEM)
    return pl.pallas_call(
        functools.partial(baseline_kernel, last),
        out_shape=jax.ShapeDtypeStruct(
            (count // LANES, rows, LANES), jnp.bfloat16 if last else jnp.float32
        ),
        in_specs=[pl.BlockSpec(memory_space=pltpu.SMEM), vmem] + [vmem] * last,
        out_specs=vmem,
        compiler_params=pltpu.CompilerParams(vmem_limit_bytes=32 * 2**20),
        cost_estimate=pl.CostEstimate(
            flops=4 * count * rows * NT,
            bytes_accessed=2 * values.size,
            transcendentals=0,
        ),
        name="baselines",
    )(pairs, values, *([before] if last else []))


def per_device(voltages, antenna_flags, baseline_pairs):
    width = lax.axis_size("wide")
    inputs = voltages.shape[0]
    count = baseline_pairs.shape[1]
    rows = 2 * CHANNEL_COUNT // width
    if rows % 32 or inputs % 8 or count // width != LANES:
        return per_device_general(voltages, antenna_flags, baseline_pairs)
    flags = jnp.broadcast_to(antenna_flags.astype(jnp.float32)[:, None], (inputs, LANES))
    proto = prototype_table()
    table = jnp.asarray(split_transform_table(width))
    total = None
    for batch in range(2):
        sent = make_spectra(batch, voltages, flags, proto, table, width)
        received = lax.all_to_all(sent, "wide", split_axis=0, concat_axis=0, tiled=True)
        total = correlate_baselines(
            baseline_pairs, received.reshape(width * inputs, rows, NT), total
        )
    columns = lax.all_to_all(total, "wide", split_axis=0, concat_axis=0, tiled=True)
    delays = jnp.dot(
        jnp.asarray(ordered_delay_table(width)),
        columns.reshape(2 * CHANNEL_COUNT, LANES),
        preferred_element_type=jnp.float32,
    )
    return delays[:CHANNEL_COUNT] ** 2 + delays[CHANNEL_COUNT:] ** 2


def solution(mesh):
    placed = (P("wide", "groups"), P(("groups", "wide")), P())
    return jax.shard_map(
        per_device, mesh=mesh, in_specs=placed, out_specs=P("groups", "wide"), check_vma=False
    )
```

```python
import functools
import math

import jax
import jax.numpy as jnp
import ml_dtypes
import numpy as np
from jax import lax
from jax.experimental import pallas as pl
from jax.experimental.pallas import tpu as pltpu
from jax.sharding import PartitionSpec as P

INPUT_COUNT = 512
CHANNEL_COUNT = 256
TAPS = 4
NT = 128
NFFT = 512


def prototype_table():
    count = TAPS * NFFT
    positions = jnp.arange(count, dtype=jnp.float32)
    start_shift = (positions - count / 2 + 0.5) / NFFT
    hamming = 0.54 - 0.46 * jnp.cos(2 * jnp.pi * positions / (count - 1))
    return (jnp.sinc(start_shift) * hamming).reshape(TAPS, NFFT)


def filter_bank(voltages, antenna_flags, first_input, count):
    framed = voltages.astype(jnp.float32).reshape(voltages.shape[0], -1, NFFT)
    prototype = prototype_table()
    filtered = jnp.zeros((voltages.shape[0], count, NFFT), jnp.float32)
    for tap_index in range(TAPS):
        filtered = (
            filtered
            + prototype[tap_index][None, None, :]
            * framed[:, first_input + tap_index : first_input + tap_index + count, :]
        )
    return filtered * antenna_flags.astype(jnp.float32)[:, None, None]


def transform_table():
    rows_int = jnp.arange(2 * CHANNEL_COUNT, dtype=jnp.int32)
    channel = rows_int // 2
    is_real = rows_int % 2 == 0
    sample = jnp.arange(NFFT, dtype=jnp.int32)
    phase = channel[:, None] * sample[None, :] % NFFT
    angle = 2 * jnp.pi * phase.astype(jnp.float32) / NFFT
    table = jnp.where(is_real[:, None], jnp.cos(angle), -jnp.sin(angle))
    return table / math.sqrt(NFFT)


def delay_table():
    chan_int = jnp.arange(CHANNEL_COUNT, dtype=jnp.int32)
    chan_float = chan_int.astype(jnp.float32)
    base = 2 * jnp.pi * chan_float / (CHANNEL_COUNT - 1)
    window = (
        0.35875
        - 0.48829 * jnp.cos(base)
        + 0.14128 * jnp.cos(2 * base)
        - 0.01168 * jnp.cos(3 * base)
    )
    phase = chan_int[:, None] * chan_int[None, :] % CHANNEL_COUNT
    angle = 2 * jnp.pi * phase.astype(jnp.float32) / CHANNEL_COUNT
    cosine = jnp.cos(angle) * window[None, :]
    sine = jnp.sin(angle) * window[None, :]
    upper = jnp.concatenate([cosine, sine], axis=1)
    lower = jnp.concatenate([-sine, cosine], axis=1)
    table = jnp.concatenate([upper, lower], axis=0) / jnp.sqrt(jnp.sum(window * window))
    return table.astype(jnp.bfloat16)


def correlate(received):
    values = received[0]
    swapped = jnp.stack([values[:, 1], -values[:, 0]], axis=1)
    stacked = jnp.stack([values, swapped], axis=0)
    return jnp.einsum("qcrit,crjt->iqcj", stacked, values, preferred_element_type=jnp.float32)


def per_device_general(voltages, antenna_flags, baseline_pairs):
    width = lax.axis_size("wide")
    local_inputs = voltages.shape[0]
    local_channels = CHANNEL_COUNT // width
    table = transform_table()
    scale = 1.0 / math.sqrt(2 * NT)
    correlation = jnp.zeros((INPUT_COUNT, 2, local_channels, INPUT_COUNT), jnp.float32)
    for batch_index in range(2):
        filtered = filter_bank(voltages, antenna_flags, batch_index * NT, NT)
        raw = jnp.einsum(
            "kn,itn->kit",
            table,
            filtered,
            precision=lax.Precision.HIGHEST,
            preferred_element_type=jnp.float32,
        )
        correlation = correlation + correlate(
            lax.all_to_all(
                raw.astype(jnp.bfloat16).reshape(width, local_channels, 2, local_inputs, NT),
                "wide",
                split_axis=0,
                concat_axis=3,
                tiled=True,
            )
        )
    baseline_count = baseline_pairs.shape[1]
    block_size = math.gcd(baseline_count, 1024)
    first_blocks = baseline_pairs[0].reshape(baseline_count // block_size, block_size)
    second_blocks = baseline_pairs[1].reshape(baseline_count // block_size, block_size)
    input_positions = jnp.arange(INPUT_COUNT, dtype=jnp.int32)

    def select_block(indices):
        first_block, second_block = indices
        rows_taken = jnp.take(correlation, first_block, axis=0)
        selector = (input_positions[None, :] == second_block[:, None]).astype(jnp.float32)
        return jnp.sum(rows_taken * selector[:, None, None, :], axis=3)

    selected = lax.map(select_block, (first_blocks, second_blocks))
    selected = selected.reshape(baseline_count, 2, local_channels)
    picked = (jnp.transpose(selected, (1, 2, 0)) * scale).astype(jnp.bfloat16)
    regrouped = lax.all_to_all(picked, "wide", split_axis=2, concat_axis=1, tiled=True)
    column_list = regrouped.reshape(2 * CHANNEL_COUNT, regrouped.shape[2])
    delays = jnp.dot(delay_table(), column_list, preferred_element_type=jnp.float32)
    return delays[:CHANNEL_COUNT] ** 2 + delays[CHANNEL_COUNT:] ** 2


LANES = 128
HALF = NFFT // 2
PIECES = 4
STEP = 4
TOGETHER = 8


def owned_channels(width):
    each = CHANNEL_COUNT // width // 2
    owner = np.arange(width)[:, None, None]
    parity = np.arange(2)[None, :, None]
    return 2 * (owner * each + np.arange(each)[None, None, :]) + parity


def split_transform_table(width):
    channel = owned_channels(width).transpose(1, 0, 2)[:, :, None, :, None]
    angle = 2 * np.pi * (channel * np.arange(HALF) % NFFT) / NFFT
    table = np.concatenate([np.cos(angle), -np.sin(angle)], axis=2) / math.sqrt(NFFT)
    table = table.reshape(2, -1, HALF).astype(np.float32)
    high = table.astype(ml_dtypes.bfloat16)
    low = (table - high.astype(np.float32)).astype(ml_dtypes.bfloat16)
    return np.concatenate([high, high, low], axis=2)


def ordered_delay_table(width):
    chan = np.arange(CHANNEL_COUNT)
    base = 2 * np.pi * chan / (CHANNEL_COUNT - 1)
    window = (
        0.35875 - 0.48829 * np.cos(base) + 0.14128 * np.cos(2 * base) - 0.01168 * np.cos(3 * base)
    )
    angle = 2 * np.pi * (chan[:, None] * chan[None, :] % CHANNEL_COUNT) / CHANNEL_COUNT
    cosine, sine = np.cos(angle) * window, np.sin(angle) * window
    table = np.block([[cosine, sine], [-sine, cosine]]) / np.sqrt(np.sum(window * window))
    channel = owned_channels(width)[:, :, None, :]
    order = channel + CHANNEL_COUNT * np.arange(2)[None, None, :, None]
    return table[:, order.reshape(-1)].astype(np.float32).astype(ml_dtypes.bfloat16)


def spectra_kernel(batch, volts, flags, proto, table_far, out, held, filt, table, sems):
    inputs = held.shape[0]
    table_copy = pltpu.make_async_copy(table_far, table, sems.at[PIECES])
    piece = NT // PIECES
    copies = []
    for part in range(PIECES):
        frames = piece + (TAPS - 1 if part == PIECES - 1 else 0)
        copies.append(
            pltpu.make_async_copy(
                volts.at[:, pl.ds((batch * NT + part * piece) * NFFT, frames * NFFT)],
                held.at[:, pl.ds(part * piece * NFFT, frames * NFFT)],
                sems.at[part],
            )
        )
    for copy in copies:
        copy.start()
    table_copy.start()
    copies[0].wait()
    for part in range(PIECES):
        if part + 1 < PIECES:
            copies[part + 1].wait()

        @pl.loop(part * piece // STEP, (part + 1) * piece // STEP)
        def _(step):
            first = step * STEP
            flag = flags[...]
            for block in range(2):
                sides = []
                for lane in (block * LANES, HALF + block * LANES):
                    frames = [
                        held[
                            :, pl.ds(pl.multiple_of((first + f) * NFFT + lane, LANES), LANES)
                        ].astype(jnp.float32)
                        for f in range(STEP + TAPS - 1)
                    ]
                    weights = [proto[tap : tap + 1, lane : lane + LANES] for tap in range(TAPS)]
                    sides.append(
                        [
                            sum(weights[tap] * frames[u + tap] for tap in range(TAPS)) * flag
                            for u in range(STEP)
                        ]
                    )
                for u in range(STEP):
                    rows = pl.ds(pl.multiple_of((first + u) * inputs, 8), inputs)
                    filt[block, rows, :] = sides[0][u] + sides[1][u]
                    filt[2 + block, rows, :] = sides[0][u] - sides[1][u]

    table_copy.wait()
    rows_each = out.shape[2] // 2

    @pl.loop(0, inputs, unroll=2)
    def _(a):
        for parity in range(2):
            x = jnp.concatenate(
                [filt[2 * parity + b, pl.ds(a, NT, stride=inputs), :] for b in range(2)], axis=1
            )
            high = x.astype(jnp.bfloat16)
            low = (x - high.astype(jnp.float32)).astype(jnp.bfloat16)
            result = lax.dot_general(
                table[parity],
                jnp.concatenate([high, low, high], axis=1),
                (((1,), (1,)), ((), ())),
                preferred_element_type=jnp.float32,
            )
            out[:, a, parity * rows_each : (parity + 1) * rows_each, :] = result.astype(
                jnp.bfloat16
            ).reshape(out.shape[0], rows_each, NT)


def make_spectra(batch, voltages, flags, proto, table, width):
    inputs = voltages.shape[0]
    rows = 2 * CHANNEL_COUNT // width
    vmem = pl.BlockSpec(memory_space=pltpu.VMEM)
    anywhere = pl.BlockSpec(memory_space=pl.ANY)
    return pl.pallas_call(
        functools.partial(spectra_kernel, batch),
        out_shape=jax.ShapeDtypeStruct((width, inputs, rows, NT), jnp.bfloat16),
        in_specs=[anywhere, vmem, vmem, anywhere],
        out_specs=vmem,
        scratch_shapes=[
            pltpu.VMEM((inputs, (NT + TAPS - 1) * NFFT), jnp.bfloat16),
            pltpu.VMEM((4, NT * inputs, LANES), jnp.float32),
            pltpu.VMEM(table.shape, table.dtype),
            pltpu.SemaphoreType.DMA((PIECES + 1,)),
        ],
        compiler_params=pltpu.CompilerParams(vmem_limit_bytes=40 * 2**20),
        cost_estimate=pl.CostEstimate(
            flops=6 * 2 * CHANNEL_COUNT * HALF * NT * inputs,
            bytes_accessed=4 * NT * NFFT * inputs,
            transcendentals=0,
        ),
        name="spectra",
    )(voltages, flags, proto, table)


def fold(parts, shift, lane):
    first = lane & shift == 0
    return [
        jnp.where(first, u, v) + pltpu.roll(jnp.where(first, v, u), shift, 1)
        for u, v in zip(parts[::2], parts[1::2])
    ]


def baseline_kernel(last, pairs, values, *rest):
    before, out, partial = rest if last else (None, *rest)
    rows = values.shape[1]
    each = rows // 4
    lane = lax.broadcasted_iota(jnp.int32, (rows, LANES), 1)

    def products(k):
        a = values[pairs[0, k]].astype(jnp.float32)
        b = values[pairs[1, k]].astype(jnp.float32)
        terms = []
        for start in (0, 2 * each):
            a_re, a_im = a[start : start + each], a[start + each : start + 2 * each]
            b_re, b_im = b[start : start + each], b[start + each : start + 2 * each]
            terms.append(a_re * b_re + a_im * b_im)
            terms.append(a_im * b_re - a_re * b_im)
        return jnp.concatenate(terms, axis=0)

    @pl.loop(0, out.shape[0])
    def _(block):
        @pl.loop(0, LANES // TOGETHER, unroll=2)
        def _(group):
            start = block * LANES + group * TOGETHER
            parts = [products(start + at) for at in range(TOGETHER)]
            shift = 1
            while len(parts) > 1:
                parts = fold(parts, shift, lane)
                shift *= 2
            partial[group] = parts[0]

        parts = [partial[group] for group in range(LANES // TOGETHER)]
        shift = TOGETHER
        while len(parts) > 1:
            parts = fold(parts, shift, lane)
            shift *= 2
        total = parts[0]
        if last:
            total = (total + before[block]) * (1.0 / math.sqrt(2 * NT))
        out[block] = total.astype(out.dtype)


def correlate_baselines(pairs, values, before=None):
    last = before is not None
    count, rows = pairs.shape[1], values.shape[1]
    vmem = pl.BlockSpec(memory_space=pltpu.VMEM)
    return pl.pallas_call(
        functools.partial(baseline_kernel, last),
        out_shape=jax.ShapeDtypeStruct(
            (count // LANES, rows, LANES), jnp.bfloat16 if last else jnp.float32
        ),
        in_specs=[pl.BlockSpec(memory_space=pltpu.SMEM), vmem] + [vmem] * last,
        out_specs=vmem,
        scratch_shapes=[pltpu.VMEM((LANES // TOGETHER, rows, LANES), jnp.float32)],
        compiler_params=pltpu.CompilerParams(vmem_limit_bytes=32 * 2**20),
        cost_estimate=pl.CostEstimate(
            flops=4 * count * rows * NT,
            bytes_accessed=2 * values.size,
            transcendentals=0,
        ),
        name="baselines",
    )(pairs, values, *([before] if last else []))


def exchange_kernel(width, sent, out, send_sems, recv_sems, own_sem):
    me = lax.axis_index("wide")
    barrier = pltpu.get_barrier_semaphore()
    for shift in range(1, width):
        pl.semaphore_signal(
            barrier,
            inc=1,
            device_id={"wide": lax.rem(me + shift, width)},
            device_id_type=pl.DeviceIdType.MESH,
        )
    own = pltpu.make_async_copy(sent.at[me], out.at[me], own_sem)
    own.start()
    pl.semaphore_wait(barrier, width - 1)
    copies = []
    for shift in range(1, width):
        other = lax.rem(me + shift, width)
        copies.append(
            pltpu.make_async_remote_copy(
                src_ref=sent.at[other],
                dst_ref=out.at[me],
                send_sem=send_sems.at[shift],
                recv_sem=recv_sems.at[shift],
                device_id={"wide": other},
                device_id_type=pl.DeviceIdType.MESH,
            )
        )
        copies[-1].start()
    own.wait()
    for copy in copies:
        copy.wait_recv()
    for copy in copies:
        copy.wait_send()


def exchange(sent, width):
    vmem = pl.BlockSpec(memory_space=pltpu.VMEM)
    return pl.pallas_call(
        functools.partial(exchange_kernel, width),
        out_shape=jax.ShapeDtypeStruct(sent.shape, sent.dtype),
        in_specs=[vmem],
        out_specs=vmem,
        scratch_shapes=[
            pltpu.SemaphoreType.DMA((width,)),
            pltpu.SemaphoreType.DMA((width,)),
            pltpu.SemaphoreType.DMA,
        ],
        compiler_params=pltpu.CompilerParams(collective_id=0, has_side_effects=True),
        name="exchange",
    )(sent)


def per_device(voltages, antenna_flags, baseline_pairs):
    width = lax.axis_size("wide")
    inputs = voltages.shape[0]
    count = baseline_pairs.shape[1]
    rows = 2 * CHANNEL_COUNT // width
    if rows % 32 or inputs % 8 or count // width != LANES:
        return per_device_general(voltages, antenna_flags, baseline_pairs)
    flags = jnp.broadcast_to(antenna_flags.astype(jnp.float32)[:, None], (inputs, LANES))
    proto = prototype_table()
    table = jnp.asarray(split_transform_table(width))
    total = None
    for batch in range(2):
        sent = make_spectra(batch, voltages, flags, proto, table, width)
        received = lax.all_to_all(sent, "wide", split_axis=0, concat_axis=0, tiled=True)
        total = correlate_baselines(
            baseline_pairs, received.reshape(width * inputs, rows, NT), total
        )
    columns = exchange(total, width)
    delays = jnp.dot(
        jnp.asarray(ordered_delay_table(width)),
        columns.reshape(2 * CHANNEL_COUNT, LANES),
        preferred_element_type=jnp.float32,
    )
    return delays[:CHANNEL_COUNT] ** 2 + delays[CHANNEL_COUNT:] ** 2


def solution(mesh):
    placed = (P("wide", "groups"), P(("groups", "wide")), P())
    return jax.shard_map(
        per_device, mesh=mesh, in_specs=placed, out_specs=P("groups", "wide"), check_vma=False
    )
```

```python
import functools
import math

import jax
import jax.numpy as jnp
import ml_dtypes
import numpy as np
from jax import lax
from jax.experimental import pallas as pl
from jax.experimental.pallas import tpu as pltpu
from jax.sharding import PartitionSpec as P

INPUT_COUNT = 512
CHANNEL_COUNT = 256
TAPS = 4
NT = 128
NFFT = 512


def prototype_table():
    count = TAPS * NFFT
    positions = jnp.arange(count, dtype=jnp.float32)
    start_shift = (positions - count / 2 + 0.5) / NFFT
    hamming = 0.54 - 0.46 * jnp.cos(2 * jnp.pi * positions / (count - 1))
    return (jnp.sinc(start_shift) * hamming).reshape(TAPS, NFFT)


def filter_bank(voltages, antenna_flags, first_input, count):
    framed = voltages.astype(jnp.float32).reshape(voltages.shape[0], -1, NFFT)
    prototype = prototype_table()
    filtered = jnp.zeros((voltages.shape[0], count, NFFT), jnp.float32)
    for tap_index in range(TAPS):
        filtered = (
            filtered
            + prototype[tap_index][None, None, :]
            * framed[:, first_input + tap_index : first_input + tap_index + count, :]
        )
    return filtered * antenna_flags.astype(jnp.float32)[:, None, None]


def transform_table():
    rows_int = jnp.arange(2 * CHANNEL_COUNT, dtype=jnp.int32)
    channel = rows_int // 2
    is_real = rows_int % 2 == 0
    sample = jnp.arange(NFFT, dtype=jnp.int32)
    phase = channel[:, None] * sample[None, :] % NFFT
    angle = 2 * jnp.pi * phase.astype(jnp.float32) / NFFT
    table = jnp.where(is_real[:, None], jnp.cos(angle), -jnp.sin(angle))
    return table / math.sqrt(NFFT)


def delay_table():
    chan_int = jnp.arange(CHANNEL_COUNT, dtype=jnp.int32)
    chan_float = chan_int.astype(jnp.float32)
    base = 2 * jnp.pi * chan_float / (CHANNEL_COUNT - 1)
    window = (
        0.35875
        - 0.48829 * jnp.cos(base)
        + 0.14128 * jnp.cos(2 * base)
        - 0.01168 * jnp.cos(3 * base)
    )
    phase = chan_int[:, None] * chan_int[None, :] % CHANNEL_COUNT
    angle = 2 * jnp.pi * phase.astype(jnp.float32) / CHANNEL_COUNT
    cosine = jnp.cos(angle) * window[None, :]
    sine = jnp.sin(angle) * window[None, :]
    upper = jnp.concatenate([cosine, sine], axis=1)
    lower = jnp.concatenate([-sine, cosine], axis=1)
    table = jnp.concatenate([upper, lower], axis=0) / jnp.sqrt(jnp.sum(window * window))
    return table.astype(jnp.bfloat16)


def correlate(received):
    values = received[0]
    swapped = jnp.stack([values[:, 1], -values[:, 0]], axis=1)
    stacked = jnp.stack([values, swapped], axis=0)
    return jnp.einsum("qcrit,crjt->iqcj", stacked, values, preferred_element_type=jnp.float32)


def per_device_general(voltages, antenna_flags, baseline_pairs):
    width = lax.axis_size("wide")
    local_inputs = voltages.shape[0]
    local_channels = CHANNEL_COUNT // width
    table = transform_table()
    scale = 1.0 / math.sqrt(2 * NT)
    correlation = jnp.zeros((INPUT_COUNT, 2, local_channels, INPUT_COUNT), jnp.float32)
    for batch_index in range(2):
        filtered = filter_bank(voltages, antenna_flags, batch_index * NT, NT)
        raw = jnp.einsum(
            "kn,itn->kit",
            table,
            filtered,
            precision=lax.Precision.HIGHEST,
            preferred_element_type=jnp.float32,
        )
        correlation = correlation + correlate(
            lax.all_to_all(
                raw.astype(jnp.bfloat16).reshape(width, local_channels, 2, local_inputs, NT),
                "wide",
                split_axis=0,
                concat_axis=3,
                tiled=True,
            )
        )
    baseline_count = baseline_pairs.shape[1]
    block_size = math.gcd(baseline_count, 1024)
    first_blocks = baseline_pairs[0].reshape(baseline_count // block_size, block_size)
    second_blocks = baseline_pairs[1].reshape(baseline_count // block_size, block_size)
    input_positions = jnp.arange(INPUT_COUNT, dtype=jnp.int32)

    def select_block(indices):
        first_block, second_block = indices
        rows_taken = jnp.take(correlation, first_block, axis=0)
        selector = (input_positions[None, :] == second_block[:, None]).astype(jnp.float32)
        return jnp.sum(rows_taken * selector[:, None, None, :], axis=3)

    selected = lax.map(select_block, (first_blocks, second_blocks))
    selected = selected.reshape(baseline_count, 2, local_channels)
    picked = (jnp.transpose(selected, (1, 2, 0)) * scale).astype(jnp.bfloat16)
    regrouped = lax.all_to_all(picked, "wide", split_axis=2, concat_axis=1, tiled=True)
    column_list = regrouped.reshape(2 * CHANNEL_COUNT, regrouped.shape[2])
    delays = jnp.dot(delay_table(), column_list, preferred_element_type=jnp.float32)
    return delays[:CHANNEL_COUNT] ** 2 + delays[CHANNEL_COUNT:] ** 2


LANES = 128
HALF = NFFT // 2
PIECES = 4
STEP = 4
TOGETHER = 8


def owned_channels(width):
    each = CHANNEL_COUNT // width // 2
    owner = np.arange(width)[:, None, None]
    parity = np.arange(2)[None, :, None]
    return 2 * (owner * each + np.arange(each)[None, None, :]) + parity


def split_transform_table(width):
    channel = owned_channels(width).transpose(1, 0, 2)[:, :, None, :, None]
    angle = 2 * np.pi * (channel * np.arange(HALF) % NFFT) / NFFT
    table = np.concatenate([np.cos(angle), -np.sin(angle)], axis=2) / math.sqrt(NFFT)
    table = table.reshape(2, -1, HALF).astype(np.float32)
    high = table.astype(ml_dtypes.bfloat16)
    low = (table - high.astype(np.float32)).astype(ml_dtypes.bfloat16)
    return np.concatenate([high, high, low], axis=2)


def ordered_delay_table(width):
    chan = np.arange(CHANNEL_COUNT)
    base = 2 * np.pi * chan / (CHANNEL_COUNT - 1)
    window = (
        0.35875 - 0.48829 * np.cos(base) + 0.14128 * np.cos(2 * base) - 0.01168 * np.cos(3 * base)
    )
    angle = 2 * np.pi * (chan[:, None] * chan[None, :] % CHANNEL_COUNT) / CHANNEL_COUNT
    cosine, sine = np.cos(angle) * window, np.sin(angle) * window
    table = np.block([[cosine, sine], [-sine, cosine]]) / np.sqrt(np.sum(window * window))
    channel = owned_channels(width)[:, None, :, :]
    order = channel + CHANNEL_COUNT * np.arange(2)[None, :, None, None]
    return table[:, order.reshape(-1)].astype(np.float32).astype(ml_dtypes.bfloat16)


def spectra_kernel(batch, volts, flags, proto, table_far, out, held, filt, table, sems):
    inputs = held.shape[0]
    table_copy = pltpu.make_async_copy(table_far, table, sems.at[PIECES])
    piece = NT // PIECES
    copies = []
    for part in range(PIECES):
        frames = piece + (TAPS - 1 if part == PIECES - 1 else 0)
        copies.append(
            pltpu.make_async_copy(
                volts.at[:, pl.ds((batch * NT + part * piece) * NFFT, frames * NFFT)],
                held.at[:, pl.ds(part * piece * NFFT, frames * NFFT)],
                sems.at[part],
            )
        )
    for copy in copies:
        copy.start()
    table_copy.start()
    copies[0].wait()
    for part in range(PIECES):
        if part + 1 < PIECES:
            copies[part + 1].wait()

        @pl.loop(part * piece // STEP, (part + 1) * piece // STEP)
        def _(step):
            first = step * STEP
            flag = flags[...]
            for block in range(2):
                sides = []
                for lane in (block * LANES, HALF + block * LANES):
                    frames = [
                        held[
                            :, pl.ds(pl.multiple_of((first + f) * NFFT + lane, LANES), LANES)
                        ].astype(jnp.float32)
                        for f in range(STEP + TAPS - 1)
                    ]
                    weights = [proto[tap : tap + 1, lane : lane + LANES] for tap in range(TAPS)]
                    sides.append(
                        [
                            sum(weights[tap] * frames[u + tap] for tap in range(TAPS)) * flag
                            for u in range(STEP)
                        ]
                    )
                for u in range(STEP):
                    rows = pl.ds(pl.multiple_of((first + u) * inputs, 8), inputs)
                    filt[block, rows, :] = sides[0][u] + sides[1][u]
                    filt[2 + block, rows, :] = sides[0][u] - sides[1][u]

    table_copy.wait()
    width, each = out.shape[0], out.shape[2] // 4

    @pl.loop(0, inputs, unroll=2)
    def _(a):
        results = []
        for parity in range(2):
            x = jnp.concatenate(
                [filt[2 * parity + b, pl.ds(a, NT, stride=inputs), :] for b in range(2)], axis=1
            )
            high = x.astype(jnp.bfloat16)
            low = (x - high.astype(jnp.float32)).astype(jnp.bfloat16)
            result = lax.dot_general(
                table[parity],
                jnp.concatenate([high, low, high], axis=1),
                (((1,), (1,)), ((), ())),
                preferred_element_type=jnp.float32,
            )
            results.append(result.reshape(width, 2, each, NT))
        pieces = [results[parity][:, r] for r in range(2) for parity in range(2)]
        out[:, a] = jnp.concatenate(pieces, axis=1).astype(jnp.bfloat16)


def make_spectra(batch, voltages, flags, proto, table, width):
    inputs = voltages.shape[0]
    rows = 2 * CHANNEL_COUNT // width
    vmem = pl.BlockSpec(memory_space=pltpu.VMEM)
    anywhere = pl.BlockSpec(memory_space=pl.ANY)
    return pl.pallas_call(
        functools.partial(spectra_kernel, batch),
        out_shape=jax.ShapeDtypeStruct((width, inputs, rows, NT), jnp.bfloat16),
        in_specs=[anywhere, vmem, vmem, anywhere],
        out_specs=vmem,
        scratch_shapes=[
            pltpu.VMEM((inputs, (NT + TAPS - 1) * NFFT), jnp.bfloat16),
            pltpu.VMEM((4, NT * inputs, LANES), jnp.float32),
            pltpu.VMEM(table.shape, table.dtype),
            pltpu.SemaphoreType.DMA((PIECES + 1,)),
        ],
        compiler_params=pltpu.CompilerParams(vmem_limit_bytes=40 * 2**20),
        cost_estimate=pl.CostEstimate(
            flops=6 * 2 * CHANNEL_COUNT * HALF * NT * inputs,
            bytes_accessed=4 * NT * NFFT * inputs,
            transcendentals=0,
        ),
        name="spectra",
    )(voltages, flags, proto, table)


def baseline_kernel(last, pairs, values, *rest):
    before, out = rest if last else (None, rest[0])
    rows = values.shape[1]
    each = rows // 2
    lane = lax.broadcasted_iota(jnp.int32, (rows, LANES), 1)
    ones = jnp.ones((2 * LANES, LANES), jnp.bfloat16)

    def products(k):
        a, b = values[pairs[0, k]], values[pairs[1, k]]
        a_re, a_im, b_re, b_im = a[:each], a[each:], b[:each], b[each:]
        left = jnp.concatenate([a_re * b_re, a_im * b_re], axis=0)
        right = jnp.concatenate([a_im * b_im, a_re * -b_im], axis=0)
        return jnp.concatenate([left, right], axis=1)

    @pl.loop(0, out.shape[0])
    def _(block):
        def some(group, total):
            first = group * TOGETHER
            terms = [products(block * LANES + first + at) for at in range(TOGETHER)]
            sums = jnp.dot(
                jnp.concatenate(terms, axis=0), ones, preferred_element_type=jnp.float32
            )
            for at in range(TOGETHER):
                total = jnp.where(lane == first + at, sums[at * rows : (at + 1) * rows], total)
            return total

        total = lax.fori_loop(
            0, LANES // TOGETHER, some, jnp.zeros((rows, LANES), jnp.float32), unroll=2
        )
        if last:
            total = (total + before[block]) * (1.0 / math.sqrt(2 * NT))
        out[block] = total.astype(out.dtype)


def correlate_baselines(pairs, values, before=None):
    last = before is not None
    count, rows = pairs.shape[1], values.shape[1]
    vmem = pl.BlockSpec(memory_space=pltpu.VMEM)
    return pl.pallas_call(
        functools.partial(baseline_kernel, last),
        out_shape=jax.ShapeDtypeStruct(
            (count // LANES, rows, LANES), jnp.bfloat16 if last else jnp.float32
        ),
        in_specs=[pl.BlockSpec(memory_space=pltpu.SMEM), vmem] + [vmem] * last,
        out_specs=vmem,
        compiler_params=pltpu.CompilerParams(vmem_limit_bytes=32 * 2**20),
        cost_estimate=pl.CostEstimate(
            flops=4 * count * rows * NT,
            bytes_accessed=2 * values.size,
            transcendentals=0,
        ),
        name="baselines",
    )(pairs, values, *([before] if last else []))


def exchange_kernel(width, sent, out, send_sems, recv_sems, own_sem):
    me = lax.axis_index("wide")
    barrier = pltpu.get_barrier_semaphore()
    for shift in range(1, width):
        pl.semaphore_signal(
            barrier,
            inc=1,
            device_id={"wide": lax.rem(me + shift, width)},
            device_id_type=pl.DeviceIdType.MESH,
        )
    own = pltpu.make_async_copy(sent.at[me], out.at[me], own_sem)
    own.start()
    pl.semaphore_wait(barrier, width - 1)
    copies = []
    for shift in range(1, width):
        other = lax.rem(me + shift, width)
        copies.append(
            pltpu.make_async_remote_copy(
                src_ref=sent.at[other],
                dst_ref=out.at[me],
                send_sem=send_sems.at[shift],
                recv_sem=recv_sems.at[shift],
                device_id={"wide": other},
                device_id_type=pl.DeviceIdType.MESH,
            )
        )
        copies[-1].start()
    own.wait()
    for copy in copies:
        copy.wait_recv()
    for copy in copies:
        copy.wait_send()


def exchange(sent, width):
    vmem = pl.BlockSpec(memory_space=pltpu.VMEM)
    return pl.pallas_call(
        functools.partial(exchange_kernel, width),
        out_shape=jax.ShapeDtypeStruct(sent.shape, sent.dtype),
        in_specs=[vmem],
        out_specs=vmem,
        scratch_shapes=[
            pltpu.SemaphoreType.DMA((width,)),
            pltpu.SemaphoreType.DMA((width,)),
            pltpu.SemaphoreType.DMA,
        ],
        compiler_params=pltpu.CompilerParams(collective_id=0, has_side_effects=True),
        name="exchange",
    )(sent)


def per_device(voltages, antenna_flags, baseline_pairs):
    width = lax.axis_size("wide")
    inputs = voltages.shape[0]
    count = baseline_pairs.shape[1]
    rows = 2 * CHANNEL_COUNT // width
    if rows % 32 or inputs % 8 or count // width != LANES:
        return per_device_general(voltages, antenna_flags, baseline_pairs)
    flags = jnp.broadcast_to(antenna_flags.astype(jnp.float32)[:, None], (inputs, LANES))
    proto = prototype_table()
    table = jnp.asarray(split_transform_table(width))
    total = None
    for batch in range(2):
        sent = make_spectra(batch, voltages, flags, proto, table, width)
        received = lax.all_to_all(sent, "wide", split_axis=0, concat_axis=0, tiled=True)
        total = correlate_baselines(
            baseline_pairs, received.reshape(width * inputs, rows, NT), total
        )
    columns = exchange(total, width)
    delays = jnp.dot(
        jnp.asarray(ordered_delay_table(width)),
        columns.reshape(2 * CHANNEL_COUNT, LANES),
        preferred_element_type=jnp.float32,
    )
    return delays[:CHANNEL_COUNT] ** 2 + delays[CHANNEL_COUNT:] ** 2


def solution(mesh):
    placed = (P("wide", "groups"), P(("groups", "wide")), P())
    return jax.shard_map(
        per_device, mesh=mesh, in_specs=placed, out_specs=P("groups", "wide"), check_vma=False
    )
```

```python
import functools
import math

import jax
import jax.numpy as jnp
import ml_dtypes
import numpy as np
from jax import lax
from jax.experimental import pallas as pl
from jax.experimental.pallas import tpu as pltpu
from jax.sharding import PartitionSpec as P

INPUT_COUNT = 512
CHANNEL_COUNT = 256
TAPS = 4
NT = 128
NFFT = 512


def prototype_table():
    count = TAPS * NFFT
    positions = jnp.arange(count, dtype=jnp.float32)
    start_shift = (positions - count / 2 + 0.5) / NFFT
    hamming = 0.54 - 0.46 * jnp.cos(2 * jnp.pi * positions / (count - 1))
    return (jnp.sinc(start_shift) * hamming).reshape(TAPS, NFFT)


def filter_bank(voltages, antenna_flags, first_input, count):
    framed = voltages.astype(jnp.float32).reshape(voltages.shape[0], -1, NFFT)
    prototype = prototype_table()
    filtered = jnp.zeros((voltages.shape[0], count, NFFT), jnp.float32)
    for tap_index in range(TAPS):
        filtered = (
            filtered
            + prototype[tap_index][None, None, :]
            * framed[:, first_input + tap_index : first_input + tap_index + count, :]
        )
    return filtered * antenna_flags.astype(jnp.float32)[:, None, None]


def transform_table():
    rows_int = jnp.arange(2 * CHANNEL_COUNT, dtype=jnp.int32)
    channel = rows_int // 2
    is_real = rows_int % 2 == 0
    sample = jnp.arange(NFFT, dtype=jnp.int32)
    phase = channel[:, None] * sample[None, :] % NFFT
    angle = 2 * jnp.pi * phase.astype(jnp.float32) / NFFT
    table = jnp.where(is_real[:, None], jnp.cos(angle), -jnp.sin(angle))
    return table / math.sqrt(NFFT)


def delay_table():
    chan_int = jnp.arange(CHANNEL_COUNT, dtype=jnp.int32)
    chan_float = chan_int.astype(jnp.float32)
    base = 2 * jnp.pi * chan_float / (CHANNEL_COUNT - 1)
    window = (
        0.35875
        - 0.48829 * jnp.cos(base)
        + 0.14128 * jnp.cos(2 * base)
        - 0.01168 * jnp.cos(3 * base)
    )
    phase = chan_int[:, None] * chan_int[None, :] % CHANNEL_COUNT
    angle = 2 * jnp.pi * phase.astype(jnp.float32) / CHANNEL_COUNT
    cosine = jnp.cos(angle) * window[None, :]
    sine = jnp.sin(angle) * window[None, :]
    upper = jnp.concatenate([cosine, sine], axis=1)
    lower = jnp.concatenate([-sine, cosine], axis=1)
    table = jnp.concatenate([upper, lower], axis=0) / jnp.sqrt(jnp.sum(window * window))
    return table.astype(jnp.bfloat16)


def correlate(received):
    values = received[0]
    swapped = jnp.stack([values[:, 1], -values[:, 0]], axis=1)
    stacked = jnp.stack([values, swapped], axis=0)
    return jnp.einsum("qcrit,crjt->iqcj", stacked, values, preferred_element_type=jnp.float32)


def per_device_general(voltages, antenna_flags, baseline_pairs):
    width = lax.axis_size("wide")
    local_inputs = voltages.shape[0]
    local_channels = CHANNEL_COUNT // width
    table = transform_table()
    scale = 1.0 / math.sqrt(2 * NT)
    correlation = jnp.zeros((INPUT_COUNT, 2, local_channels, INPUT_COUNT), jnp.float32)
    for batch_index in range(2):
        filtered = filter_bank(voltages, antenna_flags, batch_index * NT, NT)
        raw = jnp.einsum(
            "kn,itn->kit",
            table,
            filtered,
            precision=lax.Precision.HIGHEST,
            preferred_element_type=jnp.float32,
        )
        correlation = correlation + correlate(
            lax.all_to_all(
                raw.astype(jnp.bfloat16).reshape(width, local_channels, 2, local_inputs, NT),
                "wide",
                split_axis=0,
                concat_axis=3,
                tiled=True,
            )
        )
    baseline_count = baseline_pairs.shape[1]
    block_size = math.gcd(baseline_count, 1024)
    first_blocks = baseline_pairs[0].reshape(baseline_count // block_size, block_size)
    second_blocks = baseline_pairs[1].reshape(baseline_count // block_size, block_size)
    input_positions = jnp.arange(INPUT_COUNT, dtype=jnp.int32)

    def select_block(indices):
        first_block, second_block = indices
        rows_taken = jnp.take(correlation, first_block, axis=0)
        selector = (input_positions[None, :] == second_block[:, None]).astype(jnp.float32)
        return jnp.sum(rows_taken * selector[:, None, None, :], axis=3)

    selected = lax.map(select_block, (first_blocks, second_blocks))
    selected = selected.reshape(baseline_count, 2, local_channels)
    picked = (jnp.transpose(selected, (1, 2, 0)) * scale).astype(jnp.bfloat16)
    regrouped = lax.all_to_all(picked, "wide", split_axis=2, concat_axis=1, tiled=True)
    column_list = regrouped.reshape(2 * CHANNEL_COUNT, regrouped.shape[2])
    delays = jnp.dot(delay_table(), column_list, preferred_element_type=jnp.float32)
    return delays[:CHANNEL_COUNT] ** 2 + delays[CHANNEL_COUNT:] ** 2


LANES = 128
HALF = NFFT // 2
PIECES = 4
STEP = 4
TOGETHER = 16


def owned_channels(width):
    each = CHANNEL_COUNT // width // 2
    owner = np.arange(width)[:, None, None]
    parity = np.arange(2)[None, :, None]
    return 2 * (owner * each + np.arange(each)[None, None, :]) + parity


def split_transform_table(width):
    channel = owned_channels(width).transpose(1, 0, 2)[:, :, None, :, None]
    angle = 2 * np.pi * (channel * np.arange(HALF) % NFFT) / NFFT
    table = np.concatenate([np.cos(angle), -np.sin(angle)], axis=2) / math.sqrt(NFFT)
    table = table.reshape(2, -1, HALF).astype(np.float32)
    high = table.astype(ml_dtypes.bfloat16)
    low = (table - high.astype(np.float32)).astype(ml_dtypes.bfloat16)
    return np.concatenate([high, high, low], axis=2)


def ordered_delay_table(width):
    chan = np.arange(CHANNEL_COUNT)
    base = 2 * np.pi * chan / (CHANNEL_COUNT - 1)
    window = (
        0.35875 - 0.48829 * np.cos(base) + 0.14128 * np.cos(2 * base) - 0.01168 * np.cos(3 * base)
    )
    angle = 2 * np.pi * (chan[:, None] * chan[None, :] % CHANNEL_COUNT) / CHANNEL_COUNT
    cosine, sine = np.cos(angle) * window, np.sin(angle) * window
    table = np.block([[cosine, sine], [-sine, cosine]]) / np.sqrt(np.sum(window * window))
    channel = owned_channels(width)[:, None, :, :]
    order = channel + CHANNEL_COUNT * np.arange(2)[None, :, None, None]
    return table[:, order.reshape(-1)].astype(np.float32).astype(ml_dtypes.bfloat16)


def spectra_kernel(batch, volts, flags, proto, table_far, out, held, filt, table, sems):
    inputs = held.shape[0]
    table_copy = pltpu.make_async_copy(table_far, table, sems.at[PIECES])
    piece = NT // PIECES
    copies = []
    for part in range(PIECES):
        frames = piece + (TAPS - 1 if part == PIECES - 1 else 0)
        copies.append(
            pltpu.make_async_copy(
                volts.at[:, pl.ds((batch * NT + part * piece) * NFFT, frames * NFFT)],
                held.at[:, pl.ds(part * piece * NFFT, frames * NFFT)],
                sems.at[part],
            )
        )
    for copy in copies:
        copy.start()
    table_copy.start()
    copies[0].wait()
    for part in range(PIECES):
        if part + 1 < PIECES:
            copies[part + 1].wait()

        @pl.loop(part * piece // STEP, (part + 1) * piece // STEP)
        def _(step):
            first = step * STEP
            flag = flags[...]
            for block in range(2):
                sides = []
                for lane in (block * LANES, HALF + block * LANES):
                    frames = [
                        held[
                            :, pl.ds(pl.multiple_of((first + f) * NFFT + lane, LANES), LANES)
                        ].astype(jnp.float32)
                        for f in range(STEP + TAPS - 1)
                    ]
                    weights = [proto[tap : tap + 1, lane : lane + LANES] for tap in range(TAPS)]
                    sides.append(
                        [
                            sum(weights[tap] * frames[u + tap] for tap in range(TAPS)) * flag
                            for u in range(STEP)
                        ]
                    )
                for u in range(STEP):
                    rows = pl.ds(pl.multiple_of((first + u) * inputs, 8), inputs)
                    filt[block, rows, :] = sides[0][u] + sides[1][u]
                    filt[2 + block, rows, :] = sides[0][u] - sides[1][u]

    table_copy.wait()
    width, each = out.shape[0], out.shape[2] // 4

    @pl.loop(0, inputs, unroll=2)
    def _(a):
        results = []
        for parity in range(2):
            x = jnp.concatenate(
                [filt[2 * parity + b, pl.ds(a, NT, stride=inputs), :] for b in range(2)], axis=1
            )
            high = x.astype(jnp.bfloat16)
            low = (x - high.astype(jnp.float32)).astype(jnp.bfloat16)
            result = lax.dot_general(
                table[parity],
                jnp.concatenate([high, low, high], axis=1),
                (((1,), (1,)), ((), ())),
                preferred_element_type=jnp.float32,
            )
            results.append(result.reshape(width, 2, each, NT))
        pieces = [results[parity][:, r] for r in range(2) for parity in range(2)]
        out[:, a] = jnp.concatenate(pieces, axis=1).astype(jnp.bfloat16)


def make_spectra(batch, voltages, flags, proto, table, width):
    inputs = voltages.shape[0]
    rows = 2 * CHANNEL_COUNT // width
    vmem = pl.BlockSpec(memory_space=pltpu.VMEM)
    anywhere = pl.BlockSpec(memory_space=pl.ANY)
    return pl.pallas_call(
        functools.partial(spectra_kernel, batch),
        out_shape=jax.ShapeDtypeStruct((width, inputs, rows, NT), jnp.bfloat16),
        in_specs=[anywhere, vmem, vmem, anywhere],
        out_specs=vmem,
        scratch_shapes=[
            pltpu.VMEM((inputs, (NT + TAPS - 1) * NFFT), jnp.bfloat16),
            pltpu.VMEM((4, NT * inputs, LANES), jnp.float32),
            pltpu.VMEM(table.shape, table.dtype),
            pltpu.SemaphoreType.DMA((PIECES + 1,)),
        ],
        compiler_params=pltpu.CompilerParams(vmem_limit_bytes=40 * 2**20),
        cost_estimate=pl.CostEstimate(
            flops=6 * 2 * CHANNEL_COUNT * HALF * NT * inputs,
            bytes_accessed=4 * NT * NFFT * inputs,
            transcendentals=0,
        ),
        name="spectra",
    )(voltages, flags, proto, table)


def baseline_kernel(last, pairs, values, *rest):
    before, out = rest if last else (None, rest[0])
    rows = values.shape[1]
    each = rows // 2
    lane = lax.broadcasted_iota(jnp.int32, (rows, LANES), 1)
    ones = jnp.ones((2 * LANES, LANES), jnp.bfloat16)

    def products(k):
        a, b = values[pairs[0, k]], values[pairs[1, k]]
        a_re, a_im, b_re, b_im = a[:each], a[each:], b[:each], b[each:]
        left = jnp.concatenate([a_re * b_re, a_im * b_re], axis=0)
        right = jnp.concatenate([a_im * b_im, a_re * -b_im], axis=0)
        return jnp.concatenate([left, right], axis=1)

    @pl.loop(0, out.shape[0])
    def _(block):
        def some(group, total):
            first = group * TOGETHER
            terms = [products(block * LANES + first + at) for at in range(TOGETHER)]
            sums = jnp.dot(
                jnp.concatenate(terms, axis=0), ones, preferred_element_type=jnp.float32
            )
            for at in range(TOGETHER):
                total = jnp.where(lane == first + at, sums[at * rows : (at + 1) * rows], total)
            return total

        total = lax.fori_loop(
            0, LANES // TOGETHER, some, jnp.zeros((rows, LANES), jnp.float32), unroll=2
        )
        if last:
            total = (total + before[block]) * (1.0 / math.sqrt(2 * NT))
        out[block] = total.astype(out.dtype)


def correlate_baselines(pairs, values, before=None):
    last = before is not None
    count, rows = pairs.shape[1], values.shape[1]
    vmem = pl.BlockSpec(memory_space=pltpu.VMEM)
    return pl.pallas_call(
        functools.partial(baseline_kernel, last),
        out_shape=jax.ShapeDtypeStruct(
            (count // LANES, rows, LANES), jnp.bfloat16 if last else jnp.float32
        ),
        in_specs=[pl.BlockSpec(memory_space=pltpu.SMEM), vmem] + [vmem] * last,
        out_specs=vmem,
        compiler_params=pltpu.CompilerParams(vmem_limit_bytes=32 * 2**20),
        cost_estimate=pl.CostEstimate(
            flops=4 * count * rows * NT,
            bytes_accessed=2 * values.size,
            transcendentals=0,
        ),
        name="baselines",
    )(pairs, values, *([before] if last else []))


def exchange_kernel(width, sent, out, send_sems, recv_sems, own_sem):
    me = lax.axis_index("wide")
    barrier = pltpu.get_barrier_semaphore()
    for shift in range(1, width):
        pl.semaphore_signal(
            barrier,
            inc=1,
            device_id={"wide": lax.rem(me + shift, width)},
            device_id_type=pl.DeviceIdType.MESH,
        )
    own = pltpu.make_async_copy(sent.at[me], out.at[me], own_sem)
    own.start()
    pl.semaphore_wait(barrier, width - 1)
    copies = []
    for shift in range(1, width):
        other = lax.rem(me + shift, width)
        copies.append(
            pltpu.make_async_remote_copy(
                src_ref=sent.at[other],
                dst_ref=out.at[me],
                send_sem=send_sems.at[shift],
                recv_sem=recv_sems.at[shift],
                device_id={"wide": other},
                device_id_type=pl.DeviceIdType.MESH,
            )
        )
        copies[-1].start()
    own.wait()
    for copy in copies:
        copy.wait_recv()
    for copy in copies:
        copy.wait_send()


def exchange(sent, width):
    vmem = pl.BlockSpec(memory_space=pltpu.VMEM)
    return pl.pallas_call(
        functools.partial(exchange_kernel, width),
        out_shape=jax.ShapeDtypeStruct(sent.shape, sent.dtype),
        in_specs=[vmem],
        out_specs=vmem,
        scratch_shapes=[
            pltpu.SemaphoreType.DMA((width,)),
            pltpu.SemaphoreType.DMA((width,)),
            pltpu.SemaphoreType.DMA,
        ],
        compiler_params=pltpu.CompilerParams(collective_id=0, has_side_effects=True),
        name="exchange",
    )(sent)


def per_device(voltages, antenna_flags, baseline_pairs):
    width = lax.axis_size("wide")
    inputs = voltages.shape[0]
    count = baseline_pairs.shape[1]
    rows = 2 * CHANNEL_COUNT // width
    if rows % 32 or inputs % 8 or count // width != LANES:
        return per_device_general(voltages, antenna_flags, baseline_pairs)
    flags = jnp.broadcast_to(antenna_flags.astype(jnp.float32)[:, None], (inputs, LANES))
    proto = prototype_table()
    table = jnp.asarray(split_transform_table(width))
    total = None
    for batch in range(2):
        sent = make_spectra(batch, voltages, flags, proto, table, width)
        received = lax.all_to_all(sent, "wide", split_axis=0, concat_axis=0, tiled=True)
        total = correlate_baselines(
            baseline_pairs, received.reshape(width * inputs, rows, NT), total
        )
    columns = exchange(total, width)
    delays = jnp.dot(
        jnp.asarray(ordered_delay_table(width)),
        columns.reshape(2 * CHANNEL_COUNT, LANES),
        preferred_element_type=jnp.float32,
    )
    return delays[:CHANNEL_COUNT] ** 2 + delays[CHANNEL_COUNT:] ** 2


def solution(mesh):
    placed = (P("wide", "groups"), P(("groups", "wide")), P())
    return jax.shard_map(
        per_device, mesh=mesh, in_specs=placed, out_specs=P("groups", "wide"), check_vma=False
    )
```
